128 devices in a mesh: group: 8 (over y, x_hi), blk: 16 (over x_lo, z, core).
Axes of the slice: x: 4 (x_hi: 2, x_lo: 2; x = x_hi * 2 + x_lo), y: 4, z: 4, core: 2. Of those that a mesh axis runs over, the one named last changes fastest.
Arguments:
- features: bfloat16 [131072, 512], P(('group', 'blk')), may hold values from -6 to 6
- tenant: int32 [131072, 1], P(('group', 'blk')), may hold values from 0 to 31; in each aligned block of 1024 rows (0 to 1023, 1024 to 2047, ...) at most 64 rows name the same one
- label: int32 [131072], P(('group', 'blk')), may hold values from 0 to 2047
- tenant_slot: int32 [32], replicated, may hold values from 0 to 31, each once
- sample: int32 [32, 16], P('group', 'blk'), may hold values from 0 to 7
- centres: bfloat16 [32, 16384, 512], P('group', 'blk'), may hold values from -6 to 6
Outputs:
- loss: float32 [131072], P(('group', 'blk'))
The draws below stay inside these ranges and needn't reach their ends.
Inputs may be any that keep to these rules, and one draw needn't show every extreme that they name: The rows of one device name at most 64 rows of one tenant; some device's rows name some tenant exactly 64 times. `tenant_slot`: A permutation of the slots.
All inputs are finite; a program needn't handle non-finite values.
Results may differ from the reference program's by a relative error of at most 0.0003.
Values may be sent and summed in bfloat16 or wider, within the bound.
A program may use at most 128 MiB of HBM per device.

```python
import math
import jax
import jax.numpy as jnp
import numpy as np
from jax import lax

D = 512
TILE = 128
TT_DEV = 8
ST_DEV = 1
ROW_DEV = 1024
TENANTS = 32
CAPT = 64
SAMP = 2048
ROWS = 131072
N_GROUP = 8
N_BLK = 16


def set_ends(drawn, rng, low, largest):
    dims = drawn.shape
    index_at = [jax.random.randint(jax.random.fold_in(rng, axis), (), 0, dims[axis]) for axis in range(len(dims))]
    drawn = drawn.at[tuple(index_at)].set(low)
    longest = dims.index(max(dims))
    index_at[longest] = (index_at[longest] + 1) % dims[longest]
    return drawn.at[tuple(index_at)].set(largest)


def block_levels(own_key, dims, cuts, smallest, top_value):
    loudness, own = 1.0, jax.random.fold_in(own_key, 6)
    for axis_at, parts in cuts:
        heights = jnp.exp(jax.random.uniform(jax.random.fold_in(own, axis_at), (parts,), jnp.float32, smallest / len(cuts), top_value / len(cuts)))
        loudness = loudness * jnp.repeat(heights, dims[axis_at] // parts).reshape([-1 if axis == axis_at else 1 for axis in range(len(dims))])
    return loudness


def shared_out(key, own, number, rows, count, top, bound, skew):
    ranking = jax.random.permutation(key, count)
    packed, common = load_shares(count, rows * top, bound, skew, True), load_shares(count, rows * top, bound, skew, False)
    places = jnp.arange(count)

    def named(tallies, offset_by):
        used = int((tallies > 0).sum())
        fixed = max(1, used // 4)
        moved = fixed + (places - fixed + offset_by * (used - fixed)) % max(1, count - fixed)
        return jnp.zeros((count,), jnp.int32).at[ranking[jnp.where(places < fixed, places, moved)]].set(jnp.asarray(tallies, jnp.int32))

    tallies = jnp.where(number % 4 == 0, named(packed, number // 4), named(common, number - number // 4 - 1))
    mixed = jax.random.permutation(jax.random.fold_in(own, 3), count)
    source_of, sink = mixed[0:count // 2 * 2:2], mixed[1:count // 2 * 2:2]
    room = jnp.minimum(tallies[source_of] - 1, bound - tallies[sink]) // 2
    room = jnp.where((source_of == ranking[0]) | (sink == ranking[0]) | (tallies[sink] == 0), 0, jnp.maximum(room, 0))
    moved = jax.random.randint(jax.random.fold_in(own, 4), (count // 2,), 0, 1 << 20) % (room + 1)
    tallies = tallies.at[source_of].add(-moved).at[sink].add(moved)
    labels = jnp.searchsorted(jnp.cumsum(tallies), jnp.arange(rows * top), side="right").astype(jnp.int32)
    listing = labels.reshape(top, rows).T
    listing = listing[jax.random.permutation(jax.random.fold_in(own, 1), rows)]
    offset_by = jax.random.randint(jax.random.fold_in(own, 2), (rows, 1), 0, top)
    return jnp.take_along_axis(listing, (jnp.arange(top)[None, :] + offset_by) % top, axis=1)


def load_shares(number_of, total, most, slope, full):
    loads = [(1 << 20) // math.isqrt(standing ** slope) + 1 for standing in range(1, number_of + 1)]
    largest = most if full else min(most, max(-(-total // number_of), total * loads[0] // sum(loads)))
    least = 1 if total - largest >= number_of - 1 else 0
    counts, spare = [largest] + [least] * (number_of - 1), total - largest - least * (number_of - 1)
    while spare > 0:
        movable = [i for i in range(1, number_of) if counts[i] < largest] or [i for i in range(1, number_of) if counts[i] < most]
        mass, left = sum([loads[i] for i in movable]), spare
        for i in movable:
            extra = min(most - counts[i], max(1, left * loads[i] // mass), spare)
            counts[i] = counts[i] + extra
            spare = spare - extra
    return np.array(counts)


def centred(own_key, extent, width, most, cuts=(), kind=jnp.bfloat16):
    gain = block_levels(own_key, extent, cuts, -0.22, 0.18) if cuts else 1.0
    entries = jax.random.normal(own_key, extent, jnp.float32) * width * gain
    return jnp.minimum(jnp.maximum(entries, -most), most).astype(kind)


def setup_inputs(seed: int = 0) -> dict:
    keys = jax.random.split(jax.random.key(seed), 7)
    features = centred(keys[0], (ROWS, D), 1.0, 6.0, ((0, 128),))
    tenant_keys = jax.random.split(jax.random.fold_in(keys[1], 1), ROWS // ROW_DEV)
    tenant_turns = jax.random.permutation(jax.random.fold_in(keys[1], 3), ROWS // ROW_DEV)
    tenant = jax.vmap(lambda own, number: shared_out(jax.random.fold_in(keys[1], 2), own, number, ROW_DEV, TENANTS, 1, CAPT, 2))(tenant_keys, tenant_turns).reshape((ROWS, 1))
    label = set_ends(jax.random.randint(keys[2], (ROWS,), 0, SAMP), jax.random.fold_in(keys[2], 1), 0, SAMP - 1).astype(jnp.int32)
    tenant_slot = jax.random.permutation(keys[3], TENANTS).astype(jnp.int32)
    sample = set_ends(jax.random.randint(keys[4], (TENANTS, N_BLK * ST_DEV), 0, TT_DEV), jax.random.fold_in(keys[4], 1), 0, TT_DEV - 1).astype(jnp.int32)
    centres = centred(keys[5], (TENANTS, N_BLK * TT_DEV * TILE, D), 1.0, 6.0, ((0, 8), (1, 16)))
    return dict(features=features, tenant=tenant, label=label, tenant_slot=tenant_slot, sample=sample, centres=centres)


logit_scale = 32.0
margin = 0.35
epsilon = 1e-06

def normalized(values):
    wide = values.astype(jnp.float32)
    return (wide * lax.rsqrt(lax.optimization_barrier(jnp.sum(wide * wide, axis=-1, keepdims=True)) + epsilon)).astype(jnp.bfloat16)

def reference(features, tenant, label, tenant_slot, sample, centres):
    unit = normalized(features)
    slot = jnp.take(tenant_slot, tenant[:, 0], axis=0).astype(jnp.int32)
    span = ST_DEV * TILE
    classes = jnp.arange(SAMP, dtype=jnp.int32)
    owner = classes // span
    inner = classes % span // TILE
    offset = classes % TILE
    limit = N_GROUP * N_BLK * CAPT

    def one_slot(index):
        tiles = jnp.take(sample[index], owner * ST_DEV + inner, axis=0).astype(jnp.int32)
        rows_of = ((owner * TT_DEV + tiles) * TILE + offset).astype(jnp.int32)
        kernel = normalized(jnp.take(centres[index], rows_of, axis=0))
        members = jnp.nonzero(slot == index, size=limit, fill_value=ROWS)[0].astype(jnp.int32)
        chosen_rows = jnp.take(unit, members, axis=0, mode='clip')
        targets = jnp.take(label, members, axis=0, mode='clip').astype(jnp.int32)
        cosine = jnp.dot(chosen_rows, kernel.T, preferred_element_type=jnp.float32)
        hit = targets[:, None] == classes[None, :]
        logits = logit_scale * (cosine - margin * hit.astype(jnp.float32))
        totals = lax.optimization_barrier(jnp.sum(jnp.exp(logits), axis=1))
        positive = lax.optimization_barrier(jnp.sum(jnp.where(hit, logits, jnp.zeros_like(logits)), axis=1))
        return (jnp.log(totals) - positive, members)
    losses, members = lax.map(one_slot, jnp.arange(TENANTS, dtype=jnp.int32))
    return jnp.zeros((ROWS,), jnp.float32).at[members.reshape(-1)].set(losses.reshape(-1), mode='drop')
```

```python
import functools
import jax
import jax.numpy as jnp
from jax import lax
from jax.experimental import pallas as pl
from jax.experimental.pallas import tpu as pltpu
from jax.sharding import PartitionSpec as P

MESH = pl.DeviceIdType.MESH
TILE = 128
WIDTH = 512
ROWS = 1024
CAP = 64
SLOTS = 32
LANES = 128
CODE = 4 * CAP
BLOCK = CODE + 16
logit_scale = 32.0
margin = 0.35
epsilon = 1e-06
LOG2E = 1.4426950408889634


def hops(d):
    return min(d, 4 - d)


CHIPS = sorted(
    [(dx, dy) for dx in range(4) for dy in range(4)],
    key=lambda d: (-hops(d[0]) - hops(d[1]), (d[0] + d[1]) % 4),
)
SELF_CHIP = CHIPS.index((0, 0))
SELF = 2 * SELF_CHIP


def normalized(values, scale):
    wide = values.astype(jnp.float32)
    inverse = lax.rsqrt(jnp.sum(wide * wide, axis=-1, keepdims=True) + epsilon)
    return (wide * inverse * scale).astype(jnp.bfloat16)


def kernel(
    slot_ref, sample_ref, tenant_ref, label_ref, feat_hbm, cent_hbm, out_ref,
    cent0, cent1, cent2, cent3, unit, snd, rcv, tiles, kern, acc_e, acc_p, lsnd, ret,
    in_sem, row_ss, row_rs, quad_ss, quad_rs, z_ss, z_rs, loss_ss, loss_rs,
):
    group, blk = lax.axis_index("group"), lax.axis_index("blk")
    y, xh = lax.div(group, 2), lax.rem(group, 2)
    xl, z, c = lax.div(blk, 8), lax.rem(lax.div(blk, 2), 4), lax.rem(blk, 2)
    x = xh * 2 + xl

    def device(x_, y_, z_, c_):
        return (y_ * 2 + lax.div(x_, 2), lax.rem(x_, 2) * 8 + z_ * 2 + c_)

    def row_peer(o):
        dx, dy = CHIPS[o // 2]
        return device(lax.rem(x + dx, 4), lax.rem(y + dy, 4), z, lax.rem(c + o % 2, 2))

    def row_source(o):
        dx, dy = CHIPS[o // 2]
        return device(lax.rem(x + 4 - dx, 4), lax.rem(y + 4 - dy, 4), z, lax.rem(c + o % 2, 2))

    def quad_peer(q):
        return device(xh * 2 + lax.rem(xl + q // 2, 2), y, z, lax.rem(c + q % 2, 2))

    def z_peer(d):
        return device(x, y, lax.rem(z + d, 4), c)

    cents = (cent0, cent1, cent2, cent3)
    loads = []
    for q in range(4):
        t = lax.rem(xl + q // 2, 2) * 2 + lax.rem(c + q % 2, 2)
        loads.append(pltpu.make_async_copy(cent_hbm.at[t], cents[q], in_sem.at[q]))
        loads[q].start()
    feat_load = pltpu.make_async_copy(feat_hbm, unit, in_sem.at[4])
    feat_load.start()

    barrier = pltpu.get_barrier_semaphore()
    others = [o for o in range(SLOTS) if o != SELF]
    for o in others:
        pl.semaphore_signal(barrier, inc=1, device_id=row_peer(o), device_id_type=MESH)
    for d in (1, 2, 3):
        pl.semaphore_signal(barrier, inc=1, device_id=z_peer(d), device_id_type=MESH)

    for q in range(4):
        t = lax.rem(xl + q // 2, 2) * 2 + lax.rem(c + q % 2, 2)
        loads[q].wait()
        block = normalized(cents[q][sample_ref[t]], logit_scale)
        if q == 0:
            kern[0, 0] = block
        else:
            tiles[q - 1] = block

    pl.semaphore_wait(barrier, len(others) + 3)

    quad = []
    for q in (2, 3, 1):
        quad.append(
            pltpu.make_async_remote_copy(
                src_ref=tiles.at[q - 1], dst_ref=kern.at[0, q], send_sem=quad_ss.at[q - 1],
                recv_sem=quad_rs.at[q - 1], device_id=quad_peer(q), device_id_type=MESH,
            )
        )
        quad[-1].start()

    z_copies = {}

    def along_z(q):
        for d in (1, 3, 2):
            z_copies[d, q] = pltpu.make_async_remote_copy(
                src_ref=kern.at[0, q], dst_ref=kern.at[d, q], send_sem=z_ss.at[d - 1, q],
                recv_sem=z_rs.at[d - 1, q], device_id=z_peer(d), device_id_type=MESH,
            )
            z_copies[d, q].start()

    along_z(0)

    tenant = tenant_ref[...]
    slot = jnp.zeros_like(tenant)
    for n in range(SLOTS):
        slot = jnp.where(tenant == n, slot_ref[n], slot)
    y_to, xh_to = lax.shift_right_logical(slot, 3), lax.shift_right_logical(slot, 2) & 1
    x_to, c_to = xh_to * 2 + (lax.shift_right_logical(slot, 1) & 1), slot & 1
    dx, dy, dc = (x_to - x + 4) & 3, (y_to - y + 4) & 3, (c_to + c) & 1
    chip = jnp.zeros_like(slot)
    for n, (a, b) in enumerate(CHIPS):
        chip = jnp.where((dx == a) & (dy == b), n, chip)
    order = chip * 2 + dc
    member = jnp.concatenate(
        [(order == n).astype(jnp.float32) for n in range(SLOTS)], axis=0
    )
    member16 = member.astype(jnp.bfloat16)
    i0 = lax.broadcasted_iota(jnp.int32, (LANES, LANES), 0)
    i1 = lax.broadcasted_iota(jnp.int32, (LANES, LANES), 1)
    before = (i0 < i1).astype(jnp.float32).astype(jnp.bfloat16)
    within = jnp.dot(member16, before, preferred_element_type=jnp.float32)
    ones = jnp.ones((LANES, LANES), jnp.bfloat16)
    totals = jnp.dot(member16, ones, preferred_element_type=jnp.float32).astype(jnp.bfloat16)
    j0 = lax.broadcasted_iota(jnp.int32, (8 * SLOTS, 8 * SLOTS), 0)
    j1 = lax.broadcasted_iota(jnp.int32, (8 * SLOTS, 8 * SLOTS), 1)
    above = ((j1 < j0) & (lax.shift_right_logical(j0, 3) == lax.shift_right_logical(j1, 3)))
    above = above.astype(jnp.float32).astype(jnp.bfloat16)
    earlier = jnp.dot(above, totals, preferred_element_type=jnp.float32)
    ranks = (member * (within + earlier)).reshape(SLOTS, 8, LANES)
    rank = jnp.sum(ranks, axis=0).astype(jnp.int32)
    position = order * CAP + rank

    def as_row(v):
        return jnp.concatenate([v[r : r + 1, :] for r in range(8)], axis=1)

    position_row = as_row(position)
    label = as_row(label_ref[...])
    code_at = lax.broadcasted_iota(jnp.int32, (16, ROWS), 0)
    codes = jnp.where(
        code_at == 0, lax.shift_right_logical(label, 7), jnp.where(code_at == 1, label & 127, 0)
    ).astype(jnp.float32).astype(jnp.bfloat16)

    feat_load.wait()
    unit[...] = normalized(unit[...], 1.0)

    rows = {}
    iota_slot = lax.broadcasted_iota(jnp.int32, (4 * CAP, 1), 0)
    for k in range(8):
        placing = (position_row == iota_slot + k * 4 * CAP).astype(jnp.float32).astype(jnp.bfloat16)
        placed = jnp.dot(placing, unit[...], preferred_element_type=jnp.float32).astype(jnp.bfloat16)
        coded = lax.dot_general(
            codes, placing, (((1,), (1,)), ((), ())), preferred_element_type=jnp.float32
        ).astype(jnp.bfloat16)
        for a in range(4):
            o = 4 * k + a
            to = rcv if o == SELF else snd
            for f in range(4):
                to[o, f * CAP : (f + 1) * CAP, :] = placed[
                    a * CAP : (a + 1) * CAP, f * LANES : (f + 1) * LANES
                ]
            to[o, CODE:BLOCK, :] = coded[:, (a // 2) * LANES : (a // 2 + 1) * LANES]
        for a in (0, 2, 1, 3):
            o = 4 * k + a
            if o != SELF:
                rows[o] = pltpu.make_async_remote_copy(
                    src_ref=snd.at[o], dst_ref=rcv.at[o], send_sem=row_ss.at[o],
                    recv_sem=row_rs.at[o], device_id=row_peer(o), device_id_type=MESH,
                )
                rows[o].start()
        if k == 0:
            quad[2].wait()
            along_z(1)
        if k == 4:
            quad[0].wait()
            along_z(2)
        if k == 5:
            quad[1].wait()
            along_z(3)

    acc_e[...] = jnp.zeros_like(acc_e)
    acc_p[...] = jnp.zeros_like(acc_p)
    lane = lax.broadcasted_iota(jnp.int32, (1, LANES), 1)
    in_tile = lax.broadcasted_iota(jnp.int32, (TILE, 4 * CAP), 0).astype(jnp.float32)

    def targets(k):
        halves = []
        for h in range(2):
            first = rcv[4 * k + 2 * h, CODE:BLOCK, :].astype(jnp.float32)
            second = rcv[4 * k + 2 * h + 1, CODE:BLOCK, :].astype(jnp.float32)
            both = jnp.where(lane < CAP, first, second)
            halves.append(both[0:1, :] * float(TILE) + both[1:2, :])
        return jnp.concatenate(halves, axis=1)

    def group_rows(k):
        return jnp.concatenate(
            [
                jnp.concatenate(
                    [rcv[4 * k + a, f * CAP : (f + 1) * CAP, :] for f in range(4)], axis=1
                )
                for a in range(4)
            ],
            axis=0,
        )

    def step(k, j):
        target = targets(k)
        block = group_rows(k)

        def half(h, carry):
            for q in range(2):
                cosine = lax.dot_general(
                    kern[j, 2 * h + q], block, (((1,), (1,)), ((), ())),
                    preferred_element_type=jnp.float32,
                )
                owner = (lax.rem(xl + h, 2) * 4 + lax.rem(z - j + 4, 4)) * 2 + lax.rem(c + q, 2)
                hit = in_tile == target - (owner * TILE).astype(jnp.float32)
                e = jnp.where(hit, 0.0, jnp.exp2(cosine * LOG2E))
                p = jnp.where(hit, cosine, 0.0)
                acc_e[k] += jnp.sum(e.reshape(TILE // 8, 8, 4 * CAP), axis=0)
                acc_p[k] += jnp.sum(p.reshape(TILE // 8, 8, 4 * CAP), axis=0)
            return carry

        lax.fori_loop(0, 2, half, 0)

    def steps(ks, js):
        for j in js:
            lax.fori_loop(ks[0], ks[1], lambda k, carry: (step(k, j), carry)[1], 0)

    def arrived(k):
        for a in range(4):
            if 4 * k + a != SELF:
                rows[4 * k + a].wait_recv()

    def z_arrived(d):
        for q in range(4):
            z_copies[d, q].wait_recv()

    losses = {}

    def finish(k):
        positive = jnp.sum(acc_p[k], axis=0, keepdims=True) - logit_scale * margin
        total = jnp.sum(acc_e[k], axis=0, keepdims=True) + jnp.exp(positive)
        loss = jnp.log(total) - positive
        for h in range(2):
            lsnd[2 * k + h] = jnp.broadcast_to(loss[:, h * LANES : (h + 1) * LANES], (8, LANES))
        for a in range(4):
            o = 4 * k + a
            if o == SELF:
                ret[o] = jnp.broadcast_to(loss[:, (a // 2) * LANES : (a // 2 + 1) * LANES], (8, LANES))
            else:
                losses[o] = pltpu.make_async_remote_copy(
                    src_ref=lsnd.at[o // 2], dst_ref=ret.at[o], send_sem=loss_ss.at[o],
                    recv_sem=loss_rs.at[o], device_id=row_source(o), device_id_type=MESH,
                )
                losses[o].start()

    for k in range(4):
        arrived(k)
        steps((k, k + 1), (0,))
    z_arrived(1)
    z_arrived(3)
    steps((0, 4), (1, 3))
    for k in range(4, 6):
        arrived(k)
        steps((k, k + 1), (0, 1, 3))
    z_arrived(2)
    steps((0, 6), (2,))
    for k in range(6):
        finish(k)
    for k in range(6, 8):
        arrived(k)
        steps((k, k + 1), (0, 1, 3, 2))
        finish(k)

    at = (order & 1) * CAP + rank
    loss_out = jnp.zeros((8, LANES), jnp.float32)
    for o in range(SLOTS):
        if o != SELF:
            losses[o].wait_recv()
        mine = jnp.take_along_axis(ret[o], at, axis=1)
        loss_out = jnp.where(order == o, mine, loss_out)
    out_ref[...] = loss_out

    for copy in [*rows.values(), *z_copies.values(), *losses.values()]:
        copy.wait_send()


def body(features, tenant, label, tenant_slot, sample, centres):
    vmem = pl.BlockSpec(memory_space=pltpu.VMEM)
    smem = pl.BlockSpec(memory_space=pltpu.SMEM)
    hbm = pl.BlockSpec(memory_space=pl.ANY)
    bf16, f32 = jnp.bfloat16, jnp.float32
    dma = pltpu.SemaphoreType.DMA
    out = pl.pallas_call(
        kernel,
        out_shape=jax.ShapeDtypeStruct((8, LANES), f32),
        in_specs=[smem, smem, vmem, vmem, hbm, hbm],
        out_specs=vmem,
        scratch_shapes=[
            *[pltpu.VMEM((8, TILE, WIDTH), bf16) for _ in range(4)],
            pltpu.VMEM((ROWS, WIDTH), bf16),
            pltpu.VMEM((SLOTS, BLOCK, LANES), bf16),
            pltpu.VMEM((SLOTS, BLOCK, LANES), bf16),
            pltpu.VMEM((3, TILE, WIDTH), bf16),
            pltpu.VMEM((4, 4, TILE, WIDTH), bf16),
            pltpu.VMEM((8, 8, 4 * CAP), f32),
            pltpu.VMEM((8, 8, 4 * CAP), f32),
            pltpu.VMEM((16, 8, LANES), f32),
            pltpu.VMEM((SLOTS, 8, LANES), f32),
            dma((5,)), dma((SLOTS,)), dma((SLOTS,)), dma((3,)), dma((3,)),
            dma((3, 4)), dma((3, 4)), dma((SLOTS,)), dma((SLOTS,)),
        ],
        compiler_params=pltpu.CompilerParams(
            collective_id=0, has_side_effects=True, vmem_limit_bytes=48 << 20
        ),
    )(
        tenant_slot, sample.reshape(4), tenant.reshape(8, LANES), label.reshape(8, LANES),
        features, centres.reshape(4, 8, TILE, WIDTH),
    )
    return out.reshape(ROWS)


def solution(mesh):
    return jax.shard_map(
        body,
        mesh=mesh,
        in_specs=(
            P(("group", "blk"), None),
            P(("group", "blk"), None),
            P(("group", "blk")),
            P(),
            P("group", "blk"),
            P("group", "blk", None),
        ),
        out_specs=P(("group", "blk")),
        check_vma=False,
    )
```

```python
import functools
import jax
import jax.numpy as jnp
from jax import lax
from jax.experimental import pallas as pl
from jax.experimental.pallas import tpu as pltpu
from jax.sharding import PartitionSpec as P

MESH = pl.DeviceIdType.MESH
TILE = 128
WIDTH = 512
ROWS = 1024
CAP = 64
SLOTS = 32
LANES = 128
CODE = 4 * CAP
BLOCK = CODE + 16
logit_scale = 32.0
margin = 0.35
epsilon = 1e-06
LOG2E = 1.4426950408889634


def hops(d):
    return min(d, 4 - d)


CHIPS = sorted(
    [(dx, dy) for dx in range(4) for dy in range(4)],
    key=lambda d: (-hops(d[0]) - hops(d[1]), (d[0] + d[1]) % 4),
)
SELF_CHIP = CHIPS.index((0, 0))
SELF = 2 * SELF_CHIP


def normalized(values, scale):
    wide = values.astype(jnp.float32)
    inverse = lax.rsqrt(jnp.sum(wide * wide, axis=-1, keepdims=True) + epsilon)
    return (wide * inverse * scale).astype(jnp.bfloat16)


def kernel(
    slot_hbm, sample_hbm, tenant_hbm, label_hbm, feat_hbm, cent_hbm, out_ref,
    slot_ref, sample_ref, tenant_ref, label_ref, cent0, cent1, cent2, cent3, unit, snd, rcv, tiles, kern, acc_e, acc_p, lsnd, ret,
    in_sem, row_ss, row_rs, quad_ss, quad_rs, z_ss, z_rs, loss_ss, loss_rs,
):
    group, blk = lax.axis_index("group"), lax.axis_index("blk")
    y, xh = lax.div(group, 2), lax.rem(group, 2)
    xl, z, c = lax.div(blk, 8), lax.rem(lax.div(blk, 2), 4), lax.rem(blk, 2)
    x = xh * 2 + xl

    def device(x_, y_, z_, c_):
        return (y_ * 2 + lax.div(x_, 2), lax.rem(x_, 2) * 8 + z_ * 2 + c_)

    def row_peer(o):
        dx, dy = CHIPS[o // 2]
        return device(lax.rem(x + dx, 4), lax.rem(y + dy, 4), z, lax.rem(c + o % 2, 2))

    def row_source(o):
        dx, dy = CHIPS[o // 2]
        return device(lax.rem(x + 4 - dx, 4), lax.rem(y + 4 - dy, 4), z, lax.rem(c + o % 2, 2))

    def quad_peer(q):
        return device(xh * 2 + lax.rem(xl + q // 2, 2), y, z, lax.rem(c + q % 2, 2))

    def z_peer(d):
        return device(x, y, lax.rem(z + d, 4), c)

    cents = (cent0, cent1, cent2, cent3)
    loads = []
    small = [
        pltpu.make_async_copy(sample_hbm, sample_ref, in_sem.at[5]),
        pltpu.make_async_copy(slot_hbm, slot_ref, in_sem.at[6]),
        pltpu.make_async_copy(tenant_hbm, tenant_ref, in_sem.at[7]),
        pltpu.make_async_copy(label_hbm, label_ref, in_sem.at[8]),
    ]
    for load in small:
        load.start()
    for q in range(4):
        t = lax.rem(xl + q // 2, 2) * 2 + lax.rem(c + q % 2, 2)
        loads.append(pltpu.make_async_copy(cent_hbm.at[t], cents[q], in_sem.at[q]))
        loads[q].start()
    feat_load = pltpu.make_async_copy(feat_hbm, unit, in_sem.at[4])
    feat_load.start()

    barrier = pltpu.get_barrier_semaphore()
    others = [o for o in range(SLOTS) if o != SELF]
    for o in others:
        pl.semaphore_signal(barrier, inc=1, device_id=row_peer(o), device_id_type=MESH)
    for d in (1, 2, 3):
        pl.semaphore_signal(barrier, inc=1, device_id=z_peer(d), device_id_type=MESH)

    for load in small[1:]:
        load.wait()
    tenant = tenant_ref[...]
    slot = jnp.zeros_like(tenant)
    for n in range(SLOTS):
        slot = jnp.where(tenant == n, slot_ref[n], slot)
    y_to, xh_to = lax.shift_right_logical(slot, 3), lax.shift_right_logical(slot, 2) & 1
    x_to, c_to = xh_to * 2 + (lax.shift_right_logical(slot, 1) & 1), slot & 1
    dx, dy, dc = (x_to - x + 4) & 3, (y_to - y + 4) & 3, (c_to + c) & 1
    chip = jnp.zeros_like(slot)
    for n, (a, b) in enumerate(CHIPS):
        chip = jnp.where((dx == a) & (dy == b), n, chip)
    order = chip * 2 + dc
    member = jnp.concatenate(
        [(order == n).astype(jnp.float32) for n in range(SLOTS)], axis=0
    )
    member16 = member.astype(jnp.bfloat16)
    i0 = lax.broadcasted_iota(jnp.int32, (LANES, LANES), 0)
    i1 = lax.broadcasted_iota(jnp.int32, (LANES, LANES), 1)
    before = (i0 < i1).astype(jnp.float32).astype(jnp.bfloat16)
    within = jnp.dot(member16, before, preferred_element_type=jnp.float32)
    ones = jnp.ones((LANES, LANES), jnp.bfloat16)
    totals = jnp.dot(member16, ones, preferred_element_type=jnp.float32).astype(jnp.bfloat16)
    j0 = lax.broadcasted_iota(jnp.int32, (8 * SLOTS, 8 * SLOTS), 0)
    j1 = lax.broadcasted_iota(jnp.int32, (8 * SLOTS, 8 * SLOTS), 1)
    above = ((j1 < j0) & (lax.shift_right_logical(j0, 3) == lax.shift_right_logical(j1, 3)))
    above = above.astype(jnp.float32).astype(jnp.bfloat16)
    earlier = jnp.dot(above, totals, preferred_element_type=jnp.float32)
    ranks = (member * (within + earlier)).reshape(SLOTS, 8, LANES)
    rank = jnp.sum(ranks, axis=0).astype(jnp.int32)
    position = order * CAP + rank

    def as_row(v):
        return jnp.concatenate([v[r : r + 1, :] for r in range(8)], axis=1)

    position_row = as_row(position)
    label = as_row(label_ref[...])
    code_at = lax.broadcasted_iota(jnp.int32, (16, ROWS), 0)
    codes = jnp.where(
        code_at == 0, lax.shift_right_logical(label, 7), jnp.where(code_at == 1, label & 127, 0)
    ).astype(jnp.float32).astype(jnp.bfloat16)

    feat_load.wait()
    unit[...] = normalized(unit[...], 1.0)


    quad = {}
    z_copies = {}

    def along_z(q):
        for d in (1, 3, 2):
            z_copies[d, q] = pltpu.make_async_remote_copy(
                src_ref=kern.at[0, q], dst_ref=kern.at[d, q], send_sem=z_ss,
                recv_sem=z_rs.at[d - 1], device_id=z_peer(d), device_id_type=MESH,
            )
            z_copies[d, q].start()

    def own_tiles():
        small[0].wait()
        for q in (2, 3, 0, 1):
            t = lax.rem(xl + q // 2, 2) * 2 + lax.rem(c + q % 2, 2)
            loads[q].wait()
            block = normalized(cents[q][sample_ref[t]], logit_scale)
            if q == 0:
                kern[0, 0] = block
                along_z(0)
                continue
            tiles[q - 1] = block
            quad[q] = pltpu.make_async_remote_copy(
                src_ref=tiles.at[q - 1], dst_ref=kern.at[0, q], send_sem=quad_ss.at[q - 1],
                recv_sem=quad_rs.at[q - 1], device_id=quad_peer(q), device_id_type=MESH,
            )
            quad[q].start()

    rows = {}
    iota_slot = lax.broadcasted_iota(jnp.int32, (4 * CAP, 1), 0)
    for k in range(8):
        placing = (position_row == iota_slot + k * 4 * CAP).astype(jnp.float32).astype(jnp.bfloat16)
        placed = jnp.dot(placing, unit[...], preferred_element_type=jnp.float32).astype(jnp.bfloat16)
        coded = lax.dot_general(
            codes, placing, (((1,), (1,)), ((), ())), preferred_element_type=jnp.float32
        ).astype(jnp.bfloat16)
        for a in range(4):
            o = 4 * k + a
            to = rcv if o == SELF else snd
            for f in range(4):
                to[o, f * CAP : (f + 1) * CAP, :] = placed[
                    a * CAP : (a + 1) * CAP, f * LANES : (f + 1) * LANES
                ]
            to[o, CODE:BLOCK, :] = coded[:, (a // 2) * LANES : (a // 2 + 1) * LANES]
        if k == 0:
            pl.semaphore_wait(barrier, len(others) + 3)
        for a in (0, 2, 1, 3):
            o = 4 * k + a
            if o != SELF:
                rows[o] = pltpu.make_async_remote_copy(
                    src_ref=snd.at[o], dst_ref=rcv.at[o], send_sem=row_ss,
                    recv_sem=row_rs.at[k], device_id=row_peer(o), device_id_type=MESH,
                )
                rows[o].start()
        if k == 0:
            own_tiles()
        if k == 1:
            quad[1].wait()
            along_z(1)
        if k == 5:
            quad[2].wait()
            along_z(2)
        if k == 6:
            quad[3].wait()
            along_z(3)

    acc_e[...] = jnp.zeros_like(acc_e)
    acc_p[...] = jnp.zeros_like(acc_p)
    lane = lax.broadcasted_iota(jnp.int32, (1, LANES), 1)
    in_tile = lax.broadcasted_iota(jnp.int32, (TILE, 4 * CAP), 0).astype(jnp.float32)

    def targets(k):
        halves = []
        for h in range(2):
            first = rcv[4 * k + 2 * h, CODE:BLOCK, :].astype(jnp.float32)
            second = rcv[4 * k + 2 * h + 1, CODE:BLOCK, :].astype(jnp.float32)
            both = jnp.where(lane < CAP, first, second)
            halves.append(both[0:1, :] * float(TILE) + both[1:2, :])
        return jnp.concatenate(halves, axis=1)

    def group_rows(k):
        return jnp.concatenate(
            [
                jnp.concatenate(
                    [rcv[4 * k + a, f * CAP : (f + 1) * CAP, :] for f in range(4)], axis=1
                )
                for a in range(4)
            ],
            axis=0,
        )

    def step(k, j):
        target = targets(k)
        block = group_rows(k)

        logits = lax.dot_general(
            kern[j].reshape(4 * TILE, WIDTH), block, (((1,), (1,)), ((), ())),
            preferred_element_type=jnp.float32,
        )
        sum_e, sum_p = acc_e[k], acc_p[k]
        for q in range(4):
            logit = logits[q * TILE : (q + 1) * TILE]
            owner = (lax.rem(xl + q // 2, 2) * 4 + lax.rem(z - j + 4, 4)) * 2 + lax.rem(c + q % 2, 2)
            hit = in_tile == target - (owner * TILE).astype(jnp.float32)
            e = jnp.where(hit, 0.0, jnp.exp2(logit * LOG2E))
            p = jnp.where(hit, logit, 0.0)
            sum_e = sum_e + jnp.sum(e.reshape(TILE // 8, 8, 4 * CAP), axis=0)
            sum_p = sum_p + jnp.sum(p.reshape(TILE // 8, 8, 4 * CAP), axis=0)
        acc_e[k] = sum_e
        acc_p[k] = sum_p

    def steps(ks, js):
        for j in js:
            lax.fori_loop(ks[0], ks[1], lambda k, carry: (step(k, j), carry)[1], 0)

    def settle(ref, sem):
        pltpu.make_async_copy(ref, ref, sem).wait()

    def arrived(k):
        settle(rcv.at[pl.ds(4 * k, 4 if k < 7 else 3)], row_rs.at[k])

    def z_arrived(d):
        settle(kern.at[d], z_rs.at[d - 1])

    losses = {}

    def finish(k):
        positive = jnp.sum(acc_p[k], axis=0, keepdims=True) - logit_scale * margin
        total = jnp.sum(acc_e[k], axis=0, keepdims=True) + jnp.exp(positive)
        loss = jnp.log(total) - positive
        for h in range(2):
            lsnd[2 * k + h] = jnp.broadcast_to(loss[:, h * LANES : (h + 1) * LANES], (8, LANES))
        for a in range(4):
            o = 4 * k + a
            if o == SELF:
                ret[o] = jnp.broadcast_to(loss[:, (a // 2) * LANES : (a // 2 + 1) * LANES], (8, LANES))
            else:
                losses[o] = pltpu.make_async_remote_copy(
                    src_ref=lsnd.at[o // 2], dst_ref=ret.at[o], send_sem=loss_ss,
                    recv_sem=loss_rs, device_id=row_source(o), device_id_type=MESH,
                )
                losses[o].start()

    for k in range(6):
        arrived(k)
        steps((k, k + 1), (0,))
    z_arrived(1)
    z_arrived(3)
    steps((0, 6), (1, 3))
    z_arrived(2)
    steps((0, 6), (2,))
    for k in range(6):
        finish(k)
    for k in range(6, 8):
        arrived(k)
        steps((k, k + 1), (0, 1, 3, 2))
        finish(k)

    settle(snd.at[pl.ds(0, SLOTS - 1)], row_ss)
    settle(kern.at[pl.ds(1, 3)], z_ss)
    at = (order & 1) * CAP + rank
    settle(ret.at[pl.ds(0, SLOTS - 1)], loss_rs)
    loss_out = jnp.zeros((8, LANES), jnp.float32)
    for o in range(SLOTS):
        mine = jnp.take_along_axis(ret[o], at, axis=1)
        loss_out = jnp.where(order == o, mine, loss_out)
    out_ref[...] = loss_out
    settle(ret.at[pl.ds(0, SLOTS - 1)], loss_ss)


def body(features, tenant, label, tenant_slot, sample, centres):
    vmem = pl.BlockSpec(memory_space=pltpu.VMEM)
    hbm = pl.BlockSpec(memory_space=pltpu.HBM)
    bf16, f32 = jnp.bfloat16, jnp.float32
    dma = pltpu.SemaphoreType.DMA
    out = pl.pallas_call(
        kernel,
        out_shape=jax.ShapeDtypeStruct((8, LANES), f32),
        in_specs=[hbm] * 6,
        out_specs=vmem,
        scratch_shapes=[
            pltpu.SMEM((SLOTS,), jnp.int32),
            pltpu.SMEM((4,), jnp.int32),
            pltpu.VMEM((8, LANES), jnp.int32),
            pltpu.VMEM((8, LANES), jnp.int32),
            *[pltpu.VMEM((8, TILE, WIDTH), bf16) for _ in range(4)],
            pltpu.VMEM((ROWS, WIDTH), bf16),
            pltpu.VMEM((SLOTS, BLOCK, LANES), bf16),
            pltpu.VMEM((SLOTS, BLOCK, LANES), bf16),
            pltpu.VMEM((3, TILE, WIDTH), bf16),
            pltpu.VMEM((4, 4, TILE, WIDTH), bf16),
            pltpu.VMEM((8, 8, 4 * CAP), f32),
            pltpu.VMEM((8, 8, 4 * CAP), f32),
            pltpu.VMEM((16, 8, LANES), f32),
            pltpu.VMEM((SLOTS, 8, LANES), f32),
            dma((9,)), dma, dma((8,)), dma((3,)), dma((3,)), dma, dma((3,)), dma, dma,
        ],
        compiler_params=pltpu.CompilerParams(
            collective_id=0, has_side_effects=True, vmem_limit_bytes=60 << 20
        ),
    )(
        tenant_slot, sample.reshape(4), tenant.reshape(8, LANES), label.reshape(8, LANES),
        features, centres.reshape(4, 8, TILE, WIDTH),
    )
    return out.reshape(ROWS)


def solution(mesh):
    return jax.shard_map(
        body,
        mesh=mesh,
        in_specs=(
            P(("group", "blk"), None),
            P(("group", "blk"), None),
            P(("group", "blk")),
            P(),
            P("group", "blk"),
            P("group", "blk", None),
        ),
        out_specs=P(("group", "blk")),
        check_vma=False,
    )
```

```python
import functools
import jax
import jax.numpy as jnp
from jax import lax
from jax.experimental import pallas as pl
from jax.experimental.pallas import tpu as pltpu
from jax.sharding import PartitionSpec as P

MESH = pl.DeviceIdType.MESH
TILE = 128
WIDTH = 512
ROWS = 1024
CAP = 64
SLOTS = 32
LANES = 128
BLOCK = 4 * CAP
logit_scale = 32.0
margin = 0.35
epsilon = 1e-06
LOG2E = 1.4426950408889634


def hops(d):
    return min(d, 4 - d)


CHIPS = sorted(
    [(dx, dy) for dx in range(4) for dy in range(4)],
    key=lambda d: (-hops(d[0]) - hops(d[1]), (d[0] + d[1]) % 4),
)
SELF_CHIP = CHIPS.index((0, 0))
SELF = 2 * SELF_CHIP
WINDOW = 4


def normalized(values, scale):
    wide = values.astype(jnp.float32)
    inverse = lax.rsqrt(jnp.sum(wide * wide, axis=-1, keepdims=True) + epsilon)
    return (wide * inverse * scale).astype(jnp.bfloat16)


def kernel(
    slot_hbm, sample_hbm, tenant_hbm, label_hbm, feat_hbm, cent_hbm, out_ref,
    slot_ref, sample_ref, tenant_ref, label_ref, cent0, cent1, cent2, cent3, unit, snd, rcv, tiles, kern, acc_e, acc_p, lsnd, ret, lab_snd, lab_rcv,
    ready, in_sem, row_ss, row_rs, lab_ss, lab_rs, quad_ss, quad_rs, z_ss, z_rs, loss_ss, loss_rs,
):
    group, blk = lax.axis_index("group"), lax.axis_index("blk")
    y, xh = lax.div(group, 2), lax.rem(group, 2)
    xl, z, c = lax.div(blk, 8), lax.rem(lax.div(blk, 2), 4), lax.rem(blk, 2)
    x = xh * 2 + xl

    def device(x_, y_, z_, c_):
        return (y_ * 2 + lax.div(x_, 2), lax.rem(x_, 2) * 8 + z_ * 2 + c_)

    def row_peer(o):
        dx, dy = CHIPS[o // 2]
        return device(lax.rem(x + dx, 4), lax.rem(y + dy, 4), z, lax.rem(c + o % 2, 2))

    def row_source(o):
        dx, dy = CHIPS[o // 2]
        return device(lax.rem(x + 4 - dx, 4), lax.rem(y + 4 - dy, 4), z, lax.rem(c + o % 2, 2))

    def quad_peer(q):
        return device(xh * 2 + lax.rem(xl + q // 2, 2), y, z, lax.rem(c + q % 2, 2))

    def z_peer(d):
        return device(x, y, lax.rem(z + d, 4), c)

    cents = (cent0, cent1, cent2, cent3)
    owners = [lax.rem(xl + q // 2, 2) * 2 + lax.rem(c + q % 2, 2) for q in range(4)]
    sample_load = pltpu.make_async_copy(sample_hbm, sample_ref, in_sem.at[5])
    loads = [
        pltpu.make_async_copy(cent_hbm.at[owners[q]], cents[q], in_sem.at[q]) for q in range(4)
    ]
    small = [
        pltpu.make_async_copy(slot_hbm, slot_ref, in_sem.at[6]),
        pltpu.make_async_copy(tenant_hbm, tenant_ref, in_sem.at[7]),
        pltpu.make_async_copy(label_hbm, label_ref, in_sem.at[8]),
    ]
    feat_load = pltpu.make_async_copy(feat_hbm, unit, in_sem.at[4])
    sample_load.start()
    loads[2].start()
    loads[3].start()

    barrier = pltpu.get_barrier_semaphore()
    along_x = [(dx, dc) for dx in range(4) for dc in range(2) if dx or dc]
    for dx, dc in along_x:
        peer = device(lax.rem(x + dx, 4), y, z, lax.rem(c + dc, 2))
        pl.semaphore_signal(barrier, inc=1, device_id=peer, device_id_type=MESH)
    y_peers = [device(x, lax.rem(y + d, 4), z, c) for d in (1, 2, 3)]
    for peer in y_peers + [z_peer(d) for d in (1, 2, 3)]:
        pl.semaphore_signal(barrier, inc=1, device_id=peer, device_id_type=MESH)
    for load in [*small, feat_load, loads[0], loads[1]]:
        load.start()

    quad = {}
    z_copies = {}

    def along_z(q):
        for d in (1, 3, 2):
            z_copies[d, q] = pltpu.make_async_remote_copy(
                src_ref=kern.at[0, q], dst_ref=kern.at[d, q], send_sem=z_ss,
                recv_sem=z_rs.at[d - 1, q // 2], device_id=z_peer(d), device_id_type=MESH,
            )
            z_copies[d, q].start()

    def own_tile(q):
        loads[q].wait()
        block = normalized(cents[q][sample_ref[owners[q]]], logit_scale)
        if q == 0:
            kern[0, 0] = block
        else:
            tiles[q - 1] = block

    def send_tile(q):
        if q == 0:
            along_z(0)
            return
        quad[q] = pltpu.make_async_remote_copy(
            src_ref=tiles.at[q - 1], dst_ref=kern.at[0, q], send_sem=quad_ss.at[q - 1],
            recv_sem=quad_rs.at[q - 1], device_id=quad_peer(q), device_id_type=MESH,
        )
        quad[q].start()

    sample_load.wait()
    own_tile(2)
    own_tile(3)
    pl.semaphore_wait(barrier, len(along_x) + 6)
    for peer in y_peers:
        pl.semaphore_signal(ready, inc=1, device_id=peer, device_id_type=MESH)
    send_tile(2)
    send_tile(3)
    for q in (0, 1):
        own_tile(q)
        send_tile(q)

    for load in small:
        load.wait()
    tenant = tenant_ref[...]
    slot = jnp.zeros_like(tenant)
    for n in range(SLOTS):
        slot = jnp.where(tenant == n, slot_ref[n], slot)
    y_to, xh_to = lax.shift_right_logical(slot, 3), lax.shift_right_logical(slot, 2) & 1
    x_to, c_to = xh_to * 2 + (lax.shift_right_logical(slot, 1) & 1), slot & 1
    dx, dy, dc = (x_to - x + 4) & 3, (y_to - y + 4) & 3, (c_to + c) & 1
    chip = jnp.zeros_like(slot)
    for n, (a, b) in enumerate(CHIPS):
        chip = jnp.where((dx == a) & (dy == b), n, chip)
    order = chip * 2 + dc
    member = jnp.concatenate(
        [(order == n).astype(jnp.float32) for n in range(SLOTS)], axis=0
    )
    member16 = member.astype(jnp.bfloat16)
    i0 = lax.broadcasted_iota(jnp.int32, (LANES, LANES), 0)
    i1 = lax.broadcasted_iota(jnp.int32, (LANES, LANES), 1)
    before = (i0 < i1).astype(jnp.float32).astype(jnp.bfloat16)
    within = jnp.dot(member16, before, preferred_element_type=jnp.float32)
    ones = jnp.ones((LANES, LANES), jnp.bfloat16)
    totals = jnp.dot(member16, ones, preferred_element_type=jnp.float32).astype(jnp.bfloat16)
    j0 = lax.broadcasted_iota(jnp.int32, (8 * SLOTS, 8 * SLOTS), 0)
    j1 = lax.broadcasted_iota(jnp.int32, (8 * SLOTS, 8 * SLOTS), 1)
    above = ((j1 < j0) & (lax.shift_right_logical(j0, 3) == lax.shift_right_logical(j1, 3)))
    above = above.astype(jnp.float32).astype(jnp.bfloat16)
    earlier = jnp.dot(above, totals, preferred_element_type=jnp.float32)
    ranks = (member * (within + earlier)).reshape(SLOTS, 8, LANES)
    rank = jnp.sum(ranks, axis=0).astype(jnp.int32)
    position = order * CAP + rank

    def as_row(v):
        return jnp.concatenate([v[r : r + 1, :] for r in range(8)], axis=1)

    position_row = as_row(position)
    label = as_row(label_ref[...])
    code_at = lax.broadcasted_iota(jnp.int32, (16, ROWS), 0)
    codes = jnp.where(
        code_at == 0, lax.shift_right_logical(label, 7), jnp.where(code_at == 1, label & 127, 0)
    ).astype(jnp.float32).astype(jnp.bfloat16)

    feat_load.wait()
    unit[...] = normalized(unit[...], 1.0)


    def send_rows(k):
        for a in (0, 2, 1, 3):
            o = 4 * k + a
            if o != SELF:
                pltpu.make_async_remote_copy(
                    src_ref=snd.at[o], dst_ref=rcv.at[o], send_sem=row_ss,
                    recv_sem=row_rs.at[k], device_id=row_peer(o), device_id_type=MESH,
                ).start()

    iota_slot = lax.broadcasted_iota(jnp.int32, (4 * CAP, 1), 0)
    for k in range(8):
        placing = (position_row == iota_slot + k * 4 * CAP).astype(jnp.float32).astype(jnp.bfloat16)
        placed = jnp.dot(placing, unit[...], preferred_element_type=jnp.float32).astype(jnp.bfloat16)
        coded = lax.dot_general(
            codes, placing, (((1,), (1,)), ((), ())), preferred_element_type=jnp.float32
        )
        classes = coded[0:1, :] * float(TILE) + coded[1:2, :]
        for h in range(2):
            lab_snd[2 * k + h] = classes[:, h * LANES : (h + 1) * LANES]
        for a in range(4):
            o = 4 * k + a
            to = rcv if o == SELF else snd
            for f in range(4):
                to[o, f * CAP : (f + 1) * CAP, :] = placed[
                    a * CAP : (a + 1) * CAP, f * LANES : (f + 1) * LANES
                ]
        if k == 0:
            pl.semaphore_wait(ready, 3)
        if k < WINDOW:
            send_rows(k)
        for a in range(4):
            o = 4 * k + a
            if o == SELF:
                lab_rcv[o] = classes[:, (a // 2) * LANES : (a // 2 + 1) * LANES]
            else:
                pltpu.make_async_remote_copy(
                    src_ref=lab_snd.at[o // 2], dst_ref=lab_rcv.at[o], send_sem=lab_ss,
                    recv_sem=lab_rs.at[k], device_id=row_peer(o), device_id_type=MESH,
                ).start()
        if k == 1:
            quad[1].wait()
            along_z(1)
        if k == 5:
            quad[2].wait()
            along_z(2)
        if k == 6:
            quad[3].wait()
            along_z(3)

    acc_e[...] = jnp.zeros_like(acc_e)
    acc_p[...] = jnp.zeros_like(acc_p)
    lane = lax.broadcasted_iota(jnp.int32, (1, LANES), 1)
    in_tile = lax.broadcasted_iota(jnp.int32, (TILE, 4 * CAP), 0).astype(jnp.float32)

    def targets(k):
        halves = []
        for h in range(2):
            first, second = lab_rcv[4 * k + 2 * h], lab_rcv[4 * k + 2 * h + 1]
            halves.append(jnp.where(lane < CAP, first, second))
        return jnp.concatenate(halves, axis=1)

    def group_rows(k):
        return jnp.concatenate(
            [
                jnp.concatenate(
                    [rcv[4 * k + a, f * CAP : (f + 1) * CAP, :] for f in range(4)], axis=1
                )
                for a in range(4)
            ],
            axis=0,
        )

    def step(k, j, halves):
        target = targets(k)
        block = group_rows(k)

        sum_e, sum_p = acc_e[k], acc_p[k]
        for q in [2 * h + a for h in halves for a in range(2)]:
            if q % 2 == 0:
                logits = lax.dot_general(
                    kern[j, q : q + 2].reshape(2 * TILE, WIDTH), block,
                    (((1,), (1,)), ((), ())), preferred_element_type=jnp.float32,
                )
            logit = logits[q % 2 * TILE : (q % 2 + 1) * TILE]
            owner = (lax.rem(xl + q // 2, 2) * 4 + lax.rem(z - j + 4, 4)) * 2 + lax.rem(c + q % 2, 2)
            hit = in_tile == target - (owner * TILE).astype(jnp.float32)
            e = jnp.where(hit, 0.0, jnp.exp2(logit * LOG2E))
            p = jnp.where(hit, logit, 0.0)
            sum_e = sum_e + jnp.sum(e.reshape(TILE // 8, 8, 4 * CAP), axis=0)
            sum_p = sum_p + jnp.sum(p.reshape(TILE // 8, 8, 4 * CAP), axis=0)
        acc_e[k] = sum_e
        acc_p[k] = sum_p

    def steps(ks, js, halves=(0, 1)):
        def one(k, carry):
            for j in js:
                step(k, j, halves)
            return carry

        lax.fori_loop(ks[0], ks[1], one, 0)

    def settle(ref, sem):
        pltpu.make_async_copy(ref, ref, sem).wait()

    def arrived(k):
        n = 4 if k < 7 else 3
        settle(lab_rcv.at[pl.ds(4 * k, n)], lab_rs.at[k])
        settle(rcv.at[pl.ds(4 * k, n)], row_rs.at[k])

    def z_arrived(d, h):
        settle(kern.at[d, pl.ds(2 * h, 2)], z_rs.at[d - 1, h])

    losses = {}

    def finish(k):
        positive = jnp.sum(acc_p[k], axis=0, keepdims=True) - logit_scale * margin
        total = jnp.sum(acc_e[k], axis=0, keepdims=True) + jnp.exp(positive)
        loss = jnp.log(total) - positive
        for h in range(2):
            lsnd[2 * k + h] = loss[:, h * LANES : (h + 1) * LANES]
        for a in range(4):
            o = 4 * k + a
            if o == SELF:
                ret[o] = loss[:, (a // 2) * LANES : (a // 2 + 1) * LANES]
            else:
                losses[o] = pltpu.make_async_remote_copy(
                    src_ref=lsnd.at[o // 2], dst_ref=ret.at[o], send_sem=loss_ss,
                    recv_sem=loss_rs, device_id=row_source(o), device_id_type=MESH,
                )
                losses[o].start()

    def next_rows(k):
        arrived(k)
        if k + WINDOW < 8:
            send_rows(k + WINDOW)

    for k in range(4):
        next_rows(k)
        steps((k, k + 1), (0,))
    for d in (1, 3, 2):
        z_arrived(d, 0)
    steps((0, 4), (1, 3, 2), (0,))
    for d in (1, 3, 2):
        z_arrived(d, 1)
    steps((0, 4), (1, 3, 2), (1,))
    for k in range(4):
        finish(k)
    for k in range(4, 8):
        next_rows(k)
        steps((k, k + 1), (0, 1, 3, 2))
        finish(k)

    settle(snd.at[pl.ds(0, SLOTS - 1)], row_ss)
    settle(lab_rcv.at[pl.ds(0, SLOTS - 1)], lab_ss)
    settle(kern.at[pl.ds(1, 3)], z_ss)
    at = (order & 1) * CAP + rank
    settle(ret.at[pl.ds(0, SLOTS - 1)], loss_rs)
    loss_out = jnp.zeros((8, LANES), jnp.float32)
    for o in range(SLOTS):
        mine = jnp.take_along_axis(jnp.broadcast_to(ret[o], (8, LANES)), at, axis=1)
        loss_out = jnp.where(order == o, mine, loss_out)
    out_ref[...] = loss_out
    settle(ret.at[pl.ds(0, SLOTS - 1)], loss_ss)


def body(features, tenant, label, tenant_slot, sample, centres):
    vmem = pl.BlockSpec(memory_space=pltpu.VMEM)
    hbm = pl.BlockSpec(memory_space=pltpu.HBM)
    bf16, f32 = jnp.bfloat16, jnp.float32
    dma = pltpu.SemaphoreType.DMA
    out = pl.pallas_call(
        kernel,
        out_shape=jax.ShapeDtypeStruct((8, LANES), f32),
        in_specs=[hbm] * 6,
        out_specs=vmem,
        scratch_shapes=[
            pltpu.SMEM((SLOTS,), jnp.int32),
            pltpu.SMEM((4,), jnp.int32),
            pltpu.VMEM((8, LANES), jnp.int32),
            pltpu.VMEM((8, LANES), jnp.int32),
            *[pltpu.VMEM((8, TILE, WIDTH), bf16) for _ in range(4)],
            pltpu.VMEM((ROWS, WIDTH), bf16),
            pltpu.VMEM((SLOTS, BLOCK, LANES), bf16),
            pltpu.VMEM((SLOTS, BLOCK, LANES), bf16),
            pltpu.VMEM((3, TILE, WIDTH), bf16),
            pltpu.VMEM((4, 4, TILE, WIDTH), bf16),
            pltpu.VMEM((8, 8, 4 * CAP), f32),
            pltpu.VMEM((8, 8, 4 * CAP), f32),
            pltpu.VMEM((16, 1, LANES), f32),
            pltpu.VMEM((SLOTS, 1, LANES), f32),
            pltpu.VMEM((16, 1, LANES), f32),
            pltpu.VMEM((SLOTS, 1, LANES), f32),
            pltpu.SemaphoreType.REGULAR,
            dma((9,)), dma, dma((8,)), dma, dma((8,)), dma((3,)), dma((3,)), dma, dma((3, 2)), dma, dma,
        ],
        compiler_params=pltpu.CompilerParams(
            collective_id=0, has_side_effects=True, vmem_limit_bytes=60 << 20
        ),
    )(
        tenant_slot, sample.reshape(4), tenant.reshape(8, LANES), label.reshape(8, LANES),
        features, centres.reshape(4, 8, TILE, WIDTH),
    )
    return out.reshape(ROWS)


def solution(mesh):
    return jax.shard_map(
        body,
        mesh=mesh,
        in_specs=(
            P(("group", "blk"), None),
            P(("group", "blk"), None),
            P(("group", "blk")),
            P(),
            P("group", "blk"),
            P("group", "blk", None),
        ),
        out_specs=P(("group", "blk")),
        check_vma=False,
    )
```

```python
import functools
import jax
import jax.numpy as jnp
from jax import lax
from jax.experimental import pallas as pl
from jax.experimental.pallas import tpu as pltpu
from jax.sharding import PartitionSpec as P

MESH = pl.DeviceIdType.MESH
TILE = 128
WIDTH = 512
ROWS = 1024
CAP = 64
SLOTS = 32
LANES = 128
BLOCK = 4 * CAP
logit_scale = 32.0
margin = 0.35
epsilon = 1e-06
LOG2E = 1.4426950408889634


def hops(d):
    return min(d, 4 - d)


CHIPS = sorted(
    [(dx, dy) for dx in range(4) for dy in range(4)],
    key=lambda d: (-hops(d[0]) - hops(d[1]), (d[0] + d[1]) % 4),
)
SELF_CHIP = CHIPS.index((0, 0))
SELF = 2 * SELF_CHIP
WINDOW = 4


def normalized(values, scale):
    wide = values.astype(jnp.float32)
    inverse = lax.rsqrt(jnp.sum(wide * wide, axis=-1, keepdims=True) + epsilon)
    return (wide * inverse * scale).astype(jnp.bfloat16)


def kernel(
    slot_hbm, sample_hbm, tenant_hbm, label_hbm, feat_hbm, cent_hbm, out_ref,
    slot_ref, sample_ref, tenant_ref, label_ref, cent0, cent1, cent2, cent3, unit, snd, rcv, tiles, kern, acc_e, acc_p, lsnd, ret, lab_snd, lab_rcv,
    ready, in_sem, row_ss, row_rs, lab_ss, lab_rs, quad_ss, quad_rs, z_ss, z_rs, loss_ss, loss_rs,
):
    group, blk = lax.axis_index("group"), lax.axis_index("blk")
    y, xh = lax.div(group, 2), lax.rem(group, 2)
    xl, z, c = lax.div(blk, 8), lax.rem(lax.div(blk, 2), 4), lax.rem(blk, 2)
    x = xh * 2 + xl

    def device(x_, y_, z_, c_):
        return (y_ * 2 + lax.div(x_, 2), lax.rem(x_, 2) * 8 + z_ * 2 + c_)

    def row_peer(o):
        dx, dy = CHIPS[o // 2]
        return device(lax.rem(x + dx, 4), lax.rem(y + dy, 4), z, lax.rem(c + o % 2, 2))

    def row_source(o):
        dx, dy = CHIPS[o // 2]
        return device(lax.rem(x + 4 - dx, 4), lax.rem(y + 4 - dy, 4), z, lax.rem(c + o % 2, 2))

    def quad_peer(q):
        return device(xh * 2 + lax.rem(xl + q // 2, 2), y, z, lax.rem(c + q % 2, 2))

    def z_peer(d):
        return device(x, y, lax.rem(z + d, 4), c)

    cents = (cent0, cent1, cent2, cent3)
    owners = [lax.rem(xl + q // 2, 2) * 2 + lax.rem(c + q % 2, 2) for q in range(4)]
    sample_load = pltpu.make_async_copy(sample_hbm, sample_ref, in_sem.at[5])
    loads = [
        pltpu.make_async_copy(cent_hbm.at[owners[q]], cents[q], in_sem.at[q]) for q in range(4)
    ]
    small = [
        pltpu.make_async_copy(slot_hbm, slot_ref, in_sem.at[6]),
        pltpu.make_async_copy(tenant_hbm, tenant_ref, in_sem.at[7]),
        pltpu.make_async_copy(label_hbm, label_ref, in_sem.at[8]),
    ]
    feat_load = pltpu.make_async_copy(feat_hbm, unit, in_sem.at[4])
    sample_load.start()
    loads[2].start()
    loads[3].start()

    barrier = pltpu.get_barrier_semaphore()
    along_x = [(dx, dc) for dx in range(4) for dc in range(2) if dx or dc]
    for dx, dc in along_x:
        peer = device(lax.rem(x + dx, 4), y, z, lax.rem(c + dc, 2))
        pl.semaphore_signal(barrier, inc=1, device_id=peer, device_id_type=MESH)
    y_peers = [device(x, lax.rem(y + d, 4), z, c) for d in (1, 2, 3)]
    for peer in y_peers + [z_peer(d) for d in (1, 2, 3)]:
        pl.semaphore_signal(barrier, inc=1, device_id=peer, device_id_type=MESH)
    for load in [*small, feat_load, loads[0], loads[1]]:
        load.start()

    quad = {}
    z_copies = {}

    def along_z(q):
        for d in (1, 3, 2):
            z_copies[d, q] = pltpu.make_async_remote_copy(
                src_ref=kern.at[0, q], dst_ref=kern.at[d, q], send_sem=z_ss,
                recv_sem=z_rs.at[d - 1, q // 2], device_id=z_peer(d), device_id_type=MESH,
            )
            z_copies[d, q].start()

    def own_tile(q):
        loads[q].wait()
        block = normalized(cents[q][sample_ref[owners[q]]], logit_scale)
        if q == 0:
            kern[0, 0] = block
        else:
            tiles[q - 1] = block

    def send_tile(q):
        if q == 0:
            along_z(0)
            return
        quad[q] = pltpu.make_async_remote_copy(
            src_ref=tiles.at[q - 1], dst_ref=kern.at[0, q], send_sem=quad_ss.at[q - 1],
            recv_sem=quad_rs.at[q - 1], device_id=quad_peer(q), device_id_type=MESH,
        )
        quad[q].start()

    sample_load.wait()
    for q in (2, 3, 0, 1):
        own_tile(q)
    for load in small:
        load.wait()
    tenant = tenant_ref[...]
    slot = jnp.zeros_like(tenant)
    for n in range(SLOTS):
        slot = jnp.where(tenant == n, slot_ref[n], slot)
    y_to, xh_to = lax.shift_right_logical(slot, 3), lax.shift_right_logical(slot, 2) & 1
    x_to, c_to = xh_to * 2 + (lax.shift_right_logical(slot, 1) & 1), slot & 1
    dx, dy, dc = (x_to - x + 4) & 3, (y_to - y + 4) & 3, (c_to + c) & 1
    chip = jnp.zeros_like(slot)
    for n, (a, b) in enumerate(CHIPS):
        chip = jnp.where((dx == a) & (dy == b), n, chip)
    order = chip * 2 + dc
    member = jnp.concatenate(
        [(order == n).astype(jnp.float32) for n in range(SLOTS)], axis=0
    )
    member16 = member.astype(jnp.bfloat16)
    i0 = lax.broadcasted_iota(jnp.int32, (LANES, LANES), 0)
    i1 = lax.broadcasted_iota(jnp.int32, (LANES, LANES), 1)
    before = (i0 < i1).astype(jnp.float32).astype(jnp.bfloat16)
    within = jnp.dot(member16, before, preferred_element_type=jnp.float32)
    ones = jnp.ones((LANES, LANES), jnp.bfloat16)
    totals = jnp.dot(member16, ones, preferred_element_type=jnp.float32).astype(jnp.bfloat16)
    j0 = lax.broadcasted_iota(jnp.int32, (8 * SLOTS, 8 * SLOTS), 0)
    j1 = lax.broadcasted_iota(jnp.int32, (8 * SLOTS, 8 * SLOTS), 1)
    above = ((j1 < j0) & (lax.shift_right_logical(j0, 3) == lax.shift_right_logical(j1, 3)))
    above = above.astype(jnp.float32).astype(jnp.bfloat16)
    earlier = jnp.dot(above, totals, preferred_element_type=jnp.float32)
    ranks = (member * (within + earlier)).reshape(SLOTS, 8, LANES)
    rank = jnp.sum(ranks, axis=0).astype(jnp.int32)
    position = order * CAP + rank

    def as_row(v):
        return jnp.concatenate([v[r : r + 1, :] for r in range(8)], axis=1)

    position_row = as_row(position)
    label = as_row(label_ref[...])
    code_at = lax.broadcasted_iota(jnp.int32, (16, ROWS), 0)
    codes = jnp.where(
        code_at == 0, lax.shift_right_logical(label, 7), jnp.where(code_at == 1, label & 127, 0)
    ).astype(jnp.float32).astype(jnp.bfloat16)

    feat_load.wait()
    unit[...] = normalized(unit[...], 1.0)


    pl.semaphore_wait(barrier, len(along_x) + 6)
    for peer in y_peers:
        pl.semaphore_signal(ready, inc=1, device_id=peer, device_id_type=MESH)
    send_tile(2)
    send_tile(3)
    for q in (0, 1):
        send_tile(q)

    def send_rows(k):
        for a in (0, 2, 1, 3):
            o = 4 * k + a
            if o != SELF:
                pltpu.make_async_remote_copy(
                    src_ref=snd.at[o], dst_ref=rcv.at[o], send_sem=row_ss,
                    recv_sem=row_rs.at[k], device_id=row_peer(o), device_id_type=MESH,
                ).start()

    iota_slot = lax.broadcasted_iota(jnp.int32, (4 * CAP, 1), 0)
    for k in range(8):
        placing = (position_row == iota_slot + k * 4 * CAP).astype(jnp.float32).astype(jnp.bfloat16)
        placed = jnp.dot(placing, unit[...], preferred_element_type=jnp.float32).astype(jnp.bfloat16)
        coded = lax.dot_general(
            codes, placing, (((1,), (1,)), ((), ())), preferred_element_type=jnp.float32
        )
        classes = coded[0:1, :] * float(TILE) + coded[1:2, :]
        for h in range(2):
            lab_snd[2 * k + h] = classes[:, h * LANES : (h + 1) * LANES]
        for a in range(4):
            o = 4 * k + a
            to = rcv if o == SELF else snd
            for f in range(4):
                to[o, f * CAP : (f + 1) * CAP, :] = placed[
                    a * CAP : (a + 1) * CAP, f * LANES : (f + 1) * LANES
                ]
        if k == 0:
            pl.semaphore_wait(ready, 3)
        for a in range(4):
            o = 4 * k + a
            if o == SELF:
                lab_rcv[o] = classes[:, (a // 2) * LANES : (a // 2 + 1) * LANES]
            else:
                pltpu.make_async_remote_copy(
                    src_ref=lab_snd.at[o // 2], dst_ref=lab_rcv.at[o], send_sem=lab_ss,
                    recv_sem=lab_rs.at[k], device_id=row_peer(o), device_id_type=MESH,
                ).start()
        if k < WINDOW:
            send_rows(k)
        if k == 1:
            quad[1].wait()
            along_z(1)
        if k == 5:
            quad[2].wait()
            along_z(2)
        if k == 6:
            quad[3].wait()
            along_z(3)

    acc_e[...] = jnp.zeros_like(acc_e)
    acc_p[...] = jnp.zeros_like(acc_p)
    lane = lax.broadcasted_iota(jnp.int32, (1, LANES), 1)
    in_tile = lax.broadcasted_iota(jnp.int32, (TILE, 4 * CAP), 0).astype(jnp.float32)

    def targets(k):
        halves = []
        for h in range(2):
            first, second = lab_rcv[4 * k + 2 * h], lab_rcv[4 * k + 2 * h + 1]
            halves.append(jnp.where(lane < CAP, first, second))
        return jnp.concatenate(halves, axis=1)

    def group_rows(k):
        return jnp.concatenate(
            [
                jnp.concatenate(
                    [rcv[4 * k + a, f * CAP : (f + 1) * CAP, :] for f in range(4)], axis=1
                )
                for a in range(4)
            ],
            axis=0,
        )

    def step(k, j, halves):
        target = targets(k)
        block = group_rows(k)

        sum_e, sum_p = acc_e[k], acc_p[k]
        for q in [2 * h + a for h in halves for a in range(2)]:
            if q % 2 == 0:
                logits = lax.dot_general(
                    kern[j, q : q + 2].reshape(2 * TILE, WIDTH), block,
                    (((1,), (1,)), ((), ())), preferred_element_type=jnp.float32,
                )
            logit = logits[q % 2 * TILE : (q % 2 + 1) * TILE]
            owner = (lax.rem(xl + q // 2, 2) * 4 + lax.rem(z - j + 4, 4)) * 2 + lax.rem(c + q % 2, 2)
            hit = in_tile == target - (owner * TILE).astype(jnp.float32)
            e = jnp.where(hit, 0.0, jnp.exp2(logit * LOG2E))
            p = jnp.where(hit, logit, 0.0)
            sum_e = sum_e + jnp.sum(e.reshape(TILE // 8, 8, 4 * CAP), axis=0)
            sum_p = sum_p + jnp.sum(p.reshape(TILE // 8, 8, 4 * CAP), axis=0)
        acc_e[k] = sum_e
        acc_p[k] = sum_p

    def steps(ks, js, halves=(0, 1)):
        def one(k, carry):
            for j in js:
                step(k, j, halves)
            return carry

        lax.fori_loop(ks[0], ks[1], one, 0)

    def settle(ref, sem):
        pltpu.make_async_copy(ref, ref, sem).wait()

    def arrived(k):
        n = 4 if k < 7 else 3
        settle(lab_rcv.at[pl.ds(4 * k, n)], lab_rs.at[k])
        settle(rcv.at[pl.ds(4 * k, n)], row_rs.at[k])

    def z_arrived(d, h):
        settle(kern.at[d, pl.ds(2 * h, 2)], z_rs.at[d - 1, h])

    losses = {}

    def finish(k):
        positive = jnp.sum(acc_p[k], axis=0, keepdims=True) - logit_scale * margin
        total = jnp.sum(acc_e[k], axis=0, keepdims=True) + jnp.exp(positive)
        loss = jnp.log(total) - positive
        for h in range(2):
            lsnd[2 * k + h] = loss[:, h * LANES : (h + 1) * LANES]
        for a in range(4):
            o = 4 * k + a
            if o == SELF:
                ret[o] = loss[:, (a // 2) * LANES : (a // 2 + 1) * LANES]
            else:
                losses[o] = pltpu.make_async_remote_copy(
                    src_ref=lsnd.at[o // 2], dst_ref=ret.at[o], send_sem=loss_ss,
                    recv_sem=loss_rs.at[k], device_id=row_source(o), device_id_type=MESH,
                )
                losses[o].start()

    def next_rows(k):
        arrived(k)
        if k + WINDOW < 8:
            send_rows(k + WINDOW)

    for k in range(4):
        next_rows(k)
        steps((k, k + 1), (0,))
    for d in (1, 3, 2):
        z_arrived(d, 0)
    steps((0, 4), (1, 3, 2), (0,))
    for d in (1, 3, 2):
        z_arrived(d, 1)
    steps((0, 4), (1, 3, 2), (1,))
    for k in range(4):
        finish(k)
    for k in range(4, 8):
        next_rows(k)
        steps((k, k + 1), (0, 1, 3, 2))
        finish(k)

    settle(snd.at[pl.ds(0, SLOTS - 1)], row_ss)
    settle(lab_rcv.at[pl.ds(0, SLOTS - 1)], lab_ss)
    settle(kern.at[pl.ds(1, 3)], z_ss)
    at = (order & 1) * CAP + rank
    loss_out = jnp.zeros((8, LANES), jnp.float32)
    for o in range(SLOTS):
        if o % 4 == 0:
            settle(ret.at[pl.ds(o, 4 if o < 28 else 3)], loss_rs.at[o // 4])
        mine = jnp.take_along_axis(jnp.broadcast_to(ret[o], (8, LANES)), at, axis=1)
        loss_out = jnp.where(order == o, mine, loss_out)
    out_ref[...] = loss_out
    settle(ret.at[pl.ds(0, SLOTS - 1)], loss_ss)


def body(features, tenant, label, tenant_slot, sample, centres):
    vmem = pl.BlockSpec(memory_space=pltpu.VMEM)
    hbm = pl.BlockSpec(memory_space=pltpu.HBM)
    bf16, f32 = jnp.bfloat16, jnp.float32
    dma = pltpu.SemaphoreType.DMA
    out = pl.pallas_call(
        kernel,
        out_shape=jax.ShapeDtypeStruct((8, LANES), f32),
        in_specs=[hbm] * 6,
        out_specs=vmem,
        scratch_shapes=[
            pltpu.SMEM((SLOTS,), jnp.int32),
            pltpu.SMEM((4,), jnp.int32),
            pltpu.VMEM((8, LANES), jnp.int32),
            pltpu.VMEM((8, LANES), jnp.int32),
            *[pltpu.VMEM((8, TILE, WIDTH), bf16) for _ in range(4)],
            pltpu.VMEM((ROWS, WIDTH), bf16),
            pltpu.VMEM((SLOTS, BLOCK, LANES), bf16),
            pltpu.VMEM((SLOTS, BLOCK, LANES), bf16),
            pltpu.VMEM((3, TILE, WIDTH), bf16),
            pltpu.VMEM((4, 4, TILE, WIDTH), bf16),
            pltpu.VMEM((8, 8, 4 * CAP), f32),
            pltpu.VMEM((8, 8, 4 * CAP), f32),
            pltpu.VMEM((16, 1, LANES), f32),
            pltpu.VMEM((SLOTS, 1, LANES), f32),
            pltpu.VMEM((16, 1, LANES), f32),
            pltpu.VMEM((SLOTS, 1, LANES), f32),
            pltpu.SemaphoreType.REGULAR,
            dma((9,)), dma, dma((8,)), dma, dma((8,)), dma((3,)), dma((3,)), dma, dma((3, 2)), dma, dma((8,)),
        ],
        compiler_params=pltpu.CompilerParams(
            collective_id=0, has_side_effects=True, vmem_limit_bytes=60 << 20
        ),
    )(
        tenant_slot, sample.reshape(4), tenant.reshape(8, LANES), label.reshape(8, LANES),
        features, centres.reshape(4, 8, TILE, WIDTH),
    )
    return out.reshape(ROWS)


def solution(mesh):
    return jax.shard_map(
        body,
        mesh=mesh,
        in_specs=(
            P(("group", "blk"), None),
            P(("group", "blk"), None),
            P(("group", "blk")),
            P(),
            P("group", "blk"),
            P("group", "blk", None),
        ),
        out_specs=P(("group", "blk")),
        check_vma=False,
    )
```

```python
import functools
import jax
import jax.numpy as jnp
from jax import lax
from jax.experimental import pallas as pl
from jax.experimental.pallas import tpu as pltpu
from jax.sharding import PartitionSpec as P

MESH = pl.DeviceIdType.MESH
TILE = 128
WIDTH = 512
ROWS = 1024
CAP = 64
SLOTS = 32
LANES = 128
BLOCK = 4 * CAP
logit_scale = 32.0
margin = 0.35
epsilon = 1e-06
LOG2E = 1.4426950408889634


def hops(d):
    return min(d, 4 - d)


CHIPS = [(2, 2), (1, 2), (2, 1), (1, 1), (1, 3), (2, 3), (3, 2), (3, 3), (3, 1), (2, 0), (0, 2), (1, 0), (0, 1), (3, 0), (0, 3), (0, 0)]
SELF_CHIP = CHIPS.index((0, 0))
SELF = 2 * SELF_CHIP
WINDOW = 4


def normalized(values, scale):
    wide = values.astype(jnp.float32)
    inverse = lax.rsqrt(jnp.sum(wide * wide, axis=-1, keepdims=True) + epsilon)
    return (wide * inverse * scale).astype(jnp.bfloat16)


def kernel(
    slot_hbm, sample_hbm, tenant_hbm, label_hbm, feat_hbm, cent_hbm, out_ref,
    slot_ref, sample_ref, tenant_ref, label_ref, cent0, cent1, cent2, cent3, unit, snd, rcv, tiles, kern, acc_e, acc_p, lsnd, ret, lab_snd, lab_rcv,
    ready, in_sem, row_ss, row_rs, lab_ss, lab_rs, quad_ss, quad_rs, z_ss, z_rs, loss_ss, loss_rs,
):
    group, blk = lax.axis_index("group"), lax.axis_index("blk")
    y, xh = lax.div(group, 2), lax.rem(group, 2)
    xl, z, c = lax.div(blk, 8), lax.rem(lax.div(blk, 2), 4), lax.rem(blk, 2)
    x = xh * 2 + xl

    def device(x_, y_, z_, c_):
        return (y_ * 2 + lax.div(x_, 2), lax.rem(x_, 2) * 8 + z_ * 2 + c_)

    def row_peer(o):
        dx, dy = CHIPS[o // 2]
        return device(lax.rem(x + dx + 2 * c * (4 - dx), 4), lax.rem(y + dy + 2 * c * (4 - dy), 4), z, lax.rem(c + o % 2, 2))

    def row_source(o):
        dx, dy = CHIPS[o // 2]
        sc = lax.rem(c + o % 2, 2)
        return device(lax.rem(x + 4 - dx + 2 * sc * dx, 4), lax.rem(y + 4 - dy + 2 * sc * dy, 4), z, sc)

    def quad_peer(q):
        return device(xh * 2 + lax.rem(xl + q // 2, 2), y, z, lax.rem(c + q % 2, 2))

    def z_peer(d):
        return device(x, y, lax.rem(z + d, 4), c)

    cents = (cent0, cent1, cent2, cent3)
    owners = [lax.rem(xl + q // 2, 2) * 2 + lax.rem(c + q % 2, 2) for q in range(4)]
    sample_load = pltpu.make_async_copy(sample_hbm, sample_ref, in_sem.at[5])
    loads = [
        pltpu.make_async_copy(cent_hbm.at[owners[q]], cents[q], in_sem.at[q]) for q in range(4)
    ]
    small = [
        pltpu.make_async_copy(slot_hbm, slot_ref, in_sem.at[6]),
        pltpu.make_async_copy(tenant_hbm, tenant_ref, in_sem.at[7]),
        pltpu.make_async_copy(label_hbm, label_ref, in_sem.at[8]),
    ]
    feat_load = pltpu.make_async_copy(feat_hbm, unit, in_sem.at[4])
    sample_load.start()
    loads[2].start()
    loads[3].start()

    barrier = pltpu.get_barrier_semaphore()
    along_x = [(dx, dc) for dx in range(4) for dc in range(2) if dx or dc]
    for dx, dc in along_x:
        peer = device(lax.rem(x + dx, 4), y, z, lax.rem(c + dc, 2))
        pl.semaphore_signal(barrier, inc=1, device_id=peer, device_id_type=MESH)
    y_peers = [device(x, lax.rem(y + d, 4), z, c) for d in (1, 2, 3)]
    for peer in y_peers + [z_peer(d) for d in (1, 2, 3)]:
        pl.semaphore_signal(barrier, inc=1, device_id=peer, device_id_type=MESH)
    for load in [*small, feat_load, loads[0], loads[1]]:
        load.start()

    quad = {}
    z_copies = {}

    def along_z(q):
        for d in (1, 3, 2):
            z_copies[d, q] = pltpu.make_async_remote_copy(
                src_ref=kern.at[0, q], dst_ref=kern.at[d, q], send_sem=z_ss,
                recv_sem=z_rs.at[d - 1, q // 2], device_id=z_peer(d), device_id_type=MESH,
            )
            z_copies[d, q].start()

    def own_tile(q):
        loads[q].wait()
        block = normalized(cents[q][sample_ref[owners[q]]], logit_scale)
        if q == 0:
            kern[0, 0] = block
        else:
            tiles[q - 1] = block

    def send_tile(q):
        if q == 0:
            along_z(0)
            return
        quad[q] = pltpu.make_async_remote_copy(
            src_ref=tiles.at[q - 1], dst_ref=kern.at[0, q], send_sem=quad_ss.at[q - 1],
            recv_sem=quad_rs.at[q - 1], device_id=quad_peer(q), device_id_type=MESH,
        )
        quad[q].start()

    sample_load.wait()
    for q in (2, 3, 0, 1):
        own_tile(q)
    for load in small:
        load.wait()
    tenant = tenant_ref[...]
    slot = jnp.zeros_like(tenant)
    for n in range(SLOTS):
        slot = jnp.where(tenant == n, slot_ref[n], slot)
    y_to, xh_to = lax.shift_right_logical(slot, 3), lax.shift_right_logical(slot, 2) & 1
    x_to, c_to = xh_to * 2 + (lax.shift_right_logical(slot, 1) & 1), slot & 1
    turn = 1 - 2 * c
    dx, dy, dc = (turn * (x_to - x) + 4) & 3, (turn * (y_to - y) + 4) & 3, (c_to + c) & 1
    chip = jnp.zeros_like(slot)
    for n, (a, b) in enumerate(CHIPS):
        chip = jnp.where((dx == a) & (dy == b), n, chip)
    order = chip * 2 + dc
    member = jnp.concatenate(
        [(order == n).astype(jnp.float32) for n in range(SLOTS)], axis=0
    )
    member16 = member.astype(jnp.bfloat16)
    i0 = lax.broadcasted_iota(jnp.int32, (LANES, LANES), 0)
    i1 = lax.broadcasted_iota(jnp.int32, (LANES, LANES), 1)
    before = (i0 < i1).astype(jnp.float32).astype(jnp.bfloat16)
    within = jnp.dot(member16, before, preferred_element_type=jnp.float32)
    ones = jnp.ones((LANES, LANES), jnp.bfloat16)
    totals = jnp.dot(member16, ones, preferred_element_type=jnp.float32).astype(jnp.bfloat16)
    j0 = lax.broadcasted_iota(jnp.int32, (8 * SLOTS, 8 * SLOTS), 0)
    j1 = lax.broadcasted_iota(jnp.int32, (8 * SLOTS, 8 * SLOTS), 1)
    above = ((j1 < j0) & (lax.shift_right_logical(j0, 3) == lax.shift_right_logical(j1, 3)))
    above = above.astype(jnp.float32).astype(jnp.bfloat16)
    earlier = jnp.dot(above, totals, preferred_element_type=jnp.float32)
    ranks = (member * (within + earlier)).reshape(SLOTS, 8, LANES)
    rank = jnp.sum(ranks, axis=0).astype(jnp.int32)
    position = order * CAP + rank

    def as_row(v):
        return jnp.concatenate([v[r : r + 1, :] for r in range(8)], axis=1)

    position_row = as_row(position)
    label = as_row(label_ref[...])
    code_at = lax.broadcasted_iota(jnp.int32, (16, ROWS), 0)
    codes = jnp.where(
        code_at == 0, lax.shift_right_logical(label, 7), jnp.where(code_at == 1, label & 127, 0)
    ).astype(jnp.float32).astype(jnp.bfloat16)

    feat_load.wait()
    unit[...] = normalized(unit[...], 1.0)


    pl.semaphore_wait(barrier, len(along_x) + 6)
    for peer in y_peers:
        pl.semaphore_signal(ready, inc=1, device_id=peer, device_id_type=MESH)
    send_tile(2)
    send_tile(3)
    for q in (0, 1):
        send_tile(q)

    def send_rows(k):
        for a in (0, 2, 1, 3):
            o = 4 * k + a
            if o != SELF:
                pltpu.make_async_remote_copy(
                    src_ref=snd.at[o], dst_ref=rcv.at[o], send_sem=row_ss,
                    recv_sem=row_rs.at[k], device_id=row_peer(o), device_id_type=MESH,
                ).start()

    iota_slot = lax.broadcasted_iota(jnp.int32, (4 * CAP, 1), 0)
    for k in range(8):
        placing = (position_row == iota_slot + k * 4 * CAP).astype(jnp.float32).astype(jnp.bfloat16)
        placed = jnp.dot(placing, unit[...], preferred_element_type=jnp.float32).astype(jnp.bfloat16)
        coded = lax.dot_general(
            codes, placing, (((1,), (1,)), ((), ())), preferred_element_type=jnp.float32
        )
        classes = coded[0:1, :] * float(TILE) + coded[1:2, :]
        for h in range(2):
            lab_snd[2 * k + h] = classes[:, h * LANES : (h + 1) * LANES]
        for a in range(4):
            o = 4 * k + a
            to = rcv if o == SELF else snd
            for f in range(4):
                to[o, f * CAP : (f + 1) * CAP, :] = placed[
                    a * CAP : (a + 1) * CAP, f * LANES : (f + 1) * LANES
                ]
        if k == 0:
            pl.semaphore_wait(ready, 3)
        for a in range(4):
            o = 4 * k + a
            if o == SELF:
                lab_rcv[o] = classes[:, (a // 2) * LANES : (a // 2 + 1) * LANES]
            else:
                pltpu.make_async_remote_copy(
                    src_ref=lab_snd.at[o // 2], dst_ref=lab_rcv.at[o], send_sem=lab_ss,
                    recv_sem=lab_rs.at[k], device_id=row_peer(o), device_id_type=MESH,
                ).start()
        if k < WINDOW:
            send_rows(k)
        if k == 1:
            quad[1].wait()
            along_z(1)
        if k == 5:
            quad[2].wait()
            along_z(2)
        if k == 6:
            quad[3].wait()
            along_z(3)

    acc_e[...] = jnp.zeros_like(acc_e)
    acc_p[...] = jnp.zeros_like(acc_p)
    lane = lax.broadcasted_iota(jnp.int32, (1, LANES), 1)
    in_tile = lax.broadcasted_iota(jnp.int32, (TILE, 4 * CAP), 0).astype(jnp.float32)

    def targets(k):
        halves = []
        for h in range(2):
            first, second = lab_rcv[4 * k + 2 * h], lab_rcv[4 * k + 2 * h + 1]
            halves.append(jnp.where(lane < CAP, first, second))
        return jnp.concatenate(halves, axis=1)

    def group_rows(k):
        return jnp.concatenate(
            [
                jnp.concatenate(
                    [rcv[4 * k + a, f * CAP : (f + 1) * CAP, :] for f in range(4)], axis=1
                )
                for a in range(4)
            ],
            axis=0,
        )

    def step(k, j, halves):
        target = targets(k)
        block = group_rows(k)

        sum_e, sum_p = acc_e[k], acc_p[k]
        for q in [2 * h + a for h in halves for a in range(2)]:
            if q % 2 == 0:
                logits = lax.dot_general(
                    kern[j, q : q + 2].reshape(2 * TILE, WIDTH), block,
                    (((1,), (1,)), ((), ())), preferred_element_type=jnp.float32,
                )
            logit = logits[q % 2 * TILE : (q % 2 + 1) * TILE]
            owner = (lax.rem(xl + q // 2, 2) * 4 + lax.rem(z - j + 4, 4)) * 2 + lax.rem(c + q % 2, 2)
            hit = in_tile == target - (owner * TILE).astype(jnp.float32)
            e = jnp.where(hit, 0.0, jnp.exp2(logit * LOG2E))
            p = jnp.where(hit, logit, 0.0)
            sum_e = sum_e + jnp.sum(e.reshape(TILE // 8, 8, 4 * CAP), axis=0)
            sum_p = sum_p + jnp.sum(p.reshape(TILE // 8, 8, 4 * CAP), axis=0)
        acc_e[k] = sum_e
        acc_p[k] = sum_p

    def steps(ks, js, halves=(0, 1)):
        def one(k, carry):
            for j in js:
                step(k, j, halves)
            return carry

        lax.fori_loop(ks[0], ks[1], one, 0)

    def settle(ref, sem):
        pltpu.make_async_copy(ref, ref, sem).wait()

    def arrived(k):
        n = 4 if k < 7 else 3
        settle(lab_rcv.at[pl.ds(4 * k, n)], lab_rs.at[k])
        settle(rcv.at[pl.ds(4 * k, n)], row_rs.at[k])

    def z_arrived(d, h):
        settle(kern.at[d, pl.ds(2 * h, 2)], z_rs.at[d - 1, h])

    losses = {}

    def finish(k):
        positive = jnp.sum(acc_p[k], axis=0, keepdims=True) - logit_scale * margin
        total = jnp.sum(acc_e[k], axis=0, keepdims=True) + jnp.exp(positive)
        loss = jnp.log(total) - positive
        for h in range(2):
            lsnd[2 * k + h] = loss[:, h * LANES : (h + 1) * LANES]
        for a in range(4):
            o = 4 * k + a
            if o == SELF:
                ret[o] = loss[:, (a // 2) * LANES : (a // 2 + 1) * LANES]
            else:
                losses[o] = pltpu.make_async_remote_copy(
                    src_ref=lsnd.at[o // 2], dst_ref=ret.at[o], send_sem=loss_ss,
                    recv_sem=loss_rs.at[k], device_id=row_source(o), device_id_type=MESH,
                )
                losses[o].start()

    def next_rows(k):
        arrived(k)
        if k + WINDOW < 8:
            send_rows(k + WINDOW)

    for k in range(4):
        next_rows(k)
        steps((k, k + 1), (0,))
    for d in (1, 3, 2):
        z_arrived(d, 0)
    steps((0, 4), (1, 3, 2), (0,))
    for d in (1, 3, 2):
        z_arrived(d, 1)
    steps((0, 4), (1, 3, 2), (1,))
    for k in range(4):
        finish(k)
    for k in range(4, 8):
        next_rows(k)
        steps((k, k + 1), (0, 1, 3, 2))
        finish(k)

    settle(snd.at[pl.ds(0, SLOTS - 1)], row_ss)
    settle(lab_rcv.at[pl.ds(0, SLOTS - 1)], lab_ss)
    settle(kern.at[pl.ds(1, 3)], z_ss)
    at = (order & 1) * CAP + rank
    loss_out = jnp.zeros((8, LANES), jnp.float32)
    for o in range(SLOTS):
        if o % 4 == 0:
            settle(ret.at[pl.ds(o, 4 if o < 28 else 3)], loss_rs.at[o // 4])
        mine = jnp.take_along_axis(jnp.broadcast_to(ret[o], (8, LANES)), at, axis=1)
        loss_out = jnp.where(order == o, mine, loss_out)
    out_ref[...] = loss_out
    settle(ret.at[pl.ds(0, SLOTS - 1)], loss_ss)


def body(features, tenant, label, tenant_slot, sample, centres):
    vmem = pl.BlockSpec(memory_space=pltpu.VMEM)
    hbm = pl.BlockSpec(memory_space=pltpu.HBM)
    bf16, f32 = jnp.bfloat16, jnp.float32
    dma = pltpu.SemaphoreType.DMA
    out = pl.pallas_call(
        kernel,
        out_shape=jax.ShapeDtypeStruct((8, LANES), f32),
        in_specs=[hbm] * 6,
        out_specs=vmem,
        scratch_shapes=[
            pltpu.SMEM((SLOTS,), jnp.int32),
            pltpu.SMEM((4,), jnp.int32),
            pltpu.VMEM((8, LANES), jnp.int32),
            pltpu.VMEM((8, LANES), jnp.int32),
            *[pltpu.VMEM((8, TILE, WIDTH), bf16) for _ in range(4)],
            pltpu.VMEM((ROWS, WIDTH), bf16),
            pltpu.VMEM((SLOTS, BLOCK, LANES), bf16),
            pltpu.VMEM((SLOTS, BLOCK, LANES), bf16),
            pltpu.VMEM((3, TILE, WIDTH), bf16),
            pltpu.VMEM((4, 4, TILE, WIDTH), bf16),
            pltpu.VMEM((8, 8, 4 * CAP), f32),
            pltpu.VMEM((8, 8, 4 * CAP), f32),
            pltpu.VMEM((16, 1, LANES), f32),
            pltpu.VMEM((SLOTS, 1, LANES), f32),
            pltpu.VMEM((16, 1, LANES), f32),
            pltpu.VMEM((SLOTS, 1, LANES), f32),
            pltpu.SemaphoreType.REGULAR,
            dma((9,)), dma, dma((8,)), dma, dma((8,)), dma((3,)), dma((3,)), dma, dma((3, 2)), dma, dma((8,)),
        ],
        compiler_params=pltpu.CompilerParams(
            collective_id=0, has_side_effects=True, vmem_limit_bytes=60 << 20
        ),
    )(
        tenant_slot, sample.reshape(4), tenant.reshape(8, LANES), label.reshape(8, LANES),
        features, centres.reshape(4, 8, TILE, WIDTH),
    )
    return out.reshape(ROWS)


def solution(mesh):
    return jax.shard_map(
        body,
        mesh=mesh,
        in_specs=(
            P(("group", "blk"), None),
            P(("group", "blk"), None),
            P(("group", "blk")),
            P(),
            P("group", "blk"),
            P("group", "blk", None),
        ),
        out_specs=P(("group", "blk")),
        check_vma=False,
    )
```
